32 devices in a mesh: loop: 8 (over y, x, core), grp: 4 (over z).
Axes of the slice: x: 2, y: 2, z: 4, core: 2. Of those that a mesh axis runs over, the one named last changes fastest.
Arguments:
- adjacency_tiles: bfloat16 [4096, 128, 128], P(('loop', 'grp')), may hold values from -0.046875 to 0.046875
- row_block: int32 [4096], P(('loop', 'grp')), may hold values from 0 to 7
- column_block: int32 [4096], P(('loop', 'grp')), may hold values from 0 to 3
- features: bfloat16 [4096, 256], P(('loop', 'grp')), may hold values from -6 to 6
- weight: bfloat16 [256, 256], replicated, may hold values from -0.375 to 0.375
- out_bias: float32 [256], replicated, may hold values from -3 to 3
Outputs:
- result: bfloat16 [4096, 256], P(('loop', 'grp'))
The draws below stay inside these ranges and needn't reach their ends.
All inputs are finite; a program needn't handle non-finite values.
Results may differ from the reference program's by a relative error of at most 0.0046.
Values may be sent and summed in bfloat16 or wider, within the bound.
A program may use at most 128 MiB of HBM per device.

```python
import math
import jax
import jax.numpy as jnp
import numpy as np
from jax import lax

TILE = 128
F = 256
TILES_DEV = 128
NODES = 4096
TILES = 4096
N_LOOP = 8
N_GRP = 4


def touch_ends(array, own_key, least, high):
    dims = array.shape
    spot = [jax.random.randint(jax.random.fold_in(own_key, axis), (), 0, dims[axis]) for axis in range(len(dims))]
    array = array.at[tuple(spot)].set(least)
    longest = dims.index(max(dims))
    spot[longest] = (spot[longest] + 1) % dims[longest]
    return array.at[tuple(spot)].set(high)


def shard_levels(rng, dims, cuts, low, largest):
    gain, own = 1.0, jax.random.fold_in(rng, 6)
    for position, parts in cuts:
        steps = jnp.exp(jax.random.uniform(jax.random.fold_in(own, position), (parts,), jnp.float32, low / len(cuts), largest / len(cuts)))
        gain = gain * jnp.repeat(steps, dims[position] // parts).reshape([-1 if axis == position else 1 for axis in range(len(dims))])
    return gain


def rank_table(count, slope):
    portions = [(1 << 20) // math.isqrt(grade ** slope) + 1 for grade in range(1, count + 1)]
    spread = 1 + sum(portions) // (1 << 30)
    return np.cumsum(np.array([max(1, weight // spread) for weight in portions]))


def skewed_ids(own_key, dims, amount, slope):
    table = rank_table(amount, slope)
    ticket = jax.random.randint(jax.random.fold_in(own_key, 1), dims, 0, int(table[amount - 1]))
    standing = jnp.searchsorted(jnp.asarray(table, jnp.int32), ticket, side="right")
    return jax.random.permutation(jax.random.fold_in(own_key, 2), amount)[standing].astype(jnp.int32)


def scatter_about(rng, dims, width, reach, split=(), kind=jnp.bfloat16):
    entries = jax.random.normal(rng, dims, jnp.float32) * width
    if len(split) > 0:
        entries = shard_levels(rng, dims, split, -0.22, 0.18) * entries
    return jnp.clip(entries, min=-reach, max=reach).astype(kind)


def setup_inputs(seed: int = 0) -> dict:
    splits = jax.random.split(jax.random.key(seed), 7)
    return {
        "adjacency_tiles": scatter_about(splits[0], (TILES, TILE, TILE), (TILE * TILES_DEV) ** -0.5, 0.046875, ((0, 32),)),
        "row_block": touch_ends(skewed_ids(splits[1], (TILES,), N_LOOP, 1), jax.random.fold_in(splits[1], 3), 0, N_LOOP - 1).astype(jnp.int32),
        "column_block": touch_ends(jax.random.randint(splits[2], (TILES,), 0, N_GRP), jax.random.fold_in(splits[2], 1), 0, N_GRP - 1).astype(jnp.int32),
        "features": scatter_about(splits[3], (NODES, F), 1.0, 6.0, ((0, 32),)),
        "weight": scatter_about(splits[4], (F, F), F ** -0.5, 0.375),
        "out_bias": scatter_about(splits[5], (F,), 0.5, 3.0, (), jnp.float32),
    }


def reference(adjacency_tiles, row_block, column_block, features, weight, out_bias):
    device_count = N_LOOP * N_GRP
    tiles_dev = adjacency_tiles.reshape(device_count, TILES_DEV, TILE, TILE)
    rows_dev = row_block.reshape(device_count, TILES_DEV)
    columns_dev = column_block.reshape(device_count, TILES_DEV)
    sections = features.reshape(N_LOOP, N_GRP, TILE, F)

    def one_device(aggregate, device_index):
        loop_index = device_index // N_GRP
        group_index = device_index % N_GRP
        section_blocks = lax.dynamic_index_in_dim(sections, loop_index, 0, keepdims=False)
        picked = jnp.take(section_blocks, columns_dev[device_index], axis=0)
        products = jnp.einsum('tij,tjf->tif', tiles_dev[device_index].astype(jnp.float32), picked.astype(jnp.float32))
        partial_value = jax.ops.segment_sum(products, rows_dev[device_index], num_segments=N_LOOP)
        current = lax.dynamic_index_in_dim(aggregate, group_index, 1, keepdims=False)
        aggregate = lax.dynamic_update_index_in_dim(aggregate, current + partial_value, group_index, 1)
        return aggregate, None

    start = jnp.zeros((N_LOOP, N_GRP, TILE, F), jnp.float32)
    aggregate, unused = lax.scan(one_device, start, jnp.arange(device_count, dtype=jnp.int32))
    aggregate = aggregate.reshape(N_LOOP * N_GRP * TILE, F).astype(jnp.bfloat16)
    mixed = jnp.dot(aggregate, weight, preferred_element_type=jnp.float32) + out_bias
    return jax.nn.relu(mixed).astype(jnp.bfloat16)
```

```python
import functools

import jax
import jax.numpy as jnp
from jax import lax
from jax.experimental import pallas as pl
from jax.experimental.pallas import tpu as pltpu
from jax.sharding import PartitionSpec as P

LANES = 128
VMEM_BYTES = 48 * 1024 * 1024


def plain(adjacency_tiles, row_block, column_block, features, weight, out_bias):
    tile_size = adjacency_tiles.shape[1]
    feat_width = features.shape[1]
    loop_count = lax.axis_size("loop")
    section_rows = lax.all_gather(features, "grp", axis=0, tiled=True)
    section_blocks = section_rows.reshape(-1, tile_size, feat_width)
    picked = jnp.take(section_blocks, column_block, axis=0)
    products = jnp.einsum(
        "tij,tjf->tif", adjacency_tiles, picked, preferred_element_type=jnp.float32
    )
    partial_value = jax.ops.segment_sum(products, row_block, num_segments=loop_count)
    received = lax.all_to_all(partial_value, "loop", split_axis=0, concat_axis=0, tiled=True)
    summed = jnp.sum(received, axis=0)
    aggregate = summed.astype(jnp.bfloat16)
    mixed = jnp.dot(aggregate, weight, preferred_element_type=jnp.float32) + out_bias
    return jax.nn.relu(mixed).astype(jnp.bfloat16)


def column_sum(mask, value):
    return jnp.sum(jnp.where(mask, value, 0), axis=0, keepdims=True)


def sort_tables(key, count):
    wide = jnp.broadcast_to(key, (count, count))
    tall = wide.T
    sub = lax.broadcasted_iota(jnp.int32, (count, count), 0)
    lane = lax.broadcasted_iota(jnp.int32, (count, count), 1)
    equal_before = column_sum((tall == wide) & (sub < lane), 1)
    place = column_sum(tall < wide, 1) + equal_before
    place_tall = jnp.broadcast_to(place, (count, count)).T
    joins_tall = jnp.broadcast_to(equal_before, (count, count)).T
    here = place_tall == lane
    order = column_sum(here, sub)
    joins = column_sum(here & (joins_tall > 0), 1)
    last = jnp.maximum(column_sum(tall <= lane, 1) - 1, 0)
    present = jnp.minimum(column_sum(tall == lane, 1), 1)
    return order, joins, last, present


def kernel(
    loops, grps, pieces,
    tiles_hbm, row_ref, col_ref, x_ref, w_ref, bias_ref, out_ref,
    tiles, table_vec, table, sums, high, low, section, outgoing, incoming, own,
    tile_sem, table_sem, xs_sem, xr_sem, ps_sem, pr_sem,
):
    count, side = tiles.shape[0], tiles.shape[1]
    halves = section.shape[0]
    width = section.shape[2]
    my_loop, my_grp = lax.axis_index("loop"), lax.axis_index("grp")
    step = count // pieces

    loads = []
    for i in range(pieces):
        span = pl.ds(i * step, step)
        loads.append(pltpu.make_async_copy(tiles_hbm.at[span], tiles.at[span], tile_sem.at[i]))
        loads[-1].start()

    barrier = pltpu.get_barrier_semaphore()
    for d in range(1, grps):
        pl.semaphore_signal(
            barrier, inc=1, device_id=(my_loop, lax.rem(my_grp + d, grps)),
            device_id_type=pl.DeviceIdType.MESH,
        )
    for d in range(1, loops):
        pl.semaphore_signal(
            barrier, inc=1, device_id=(lax.rem(my_loop + d, loops), my_grp),
            device_id_type=pl.DeviceIdType.MESH,
        )

    rows = sort_tables(row_ref[...] * grps + col_ref[...], count)
    for i, values in enumerate(rows):
        table_vec[i : i + 1, :] = values
    to_scalars = pltpu.make_async_copy(table_vec, table, table_sem)
    to_scalars.start()

    pl.semaphore_wait(barrier, grps + loops - 2)

    def slot(g):
        return pl.ds(pl.multiple_of(g * side, side), side)

    def x_copy(h, target, source):
        return pltpu.make_async_remote_copy(
            src_ref=x_ref.at[:, pl.ds(h * width, width)],
            dst_ref=section.at[h, slot(source)],
            send_sem=xs_sem.at[h, target],
            recv_sem=xr_sem.at[h, source],
            device_id=(my_loop, target),
            device_id_type=pl.DeviceIdType.MESH,
        )

    def p_copy(h, d, target, source):
        return pltpu.make_async_remote_copy(
            src_ref=outgoing.at[h, d - 1],
            dst_ref=incoming.at[h, source],
            send_sem=ps_sem.at[h, d - 1],
            recv_sem=pr_sem.at[h, source],
            device_id=(target, my_grp),
            device_id_type=pl.DeviceIdType.MESH,
        )

    for h in range(halves):
        for d in range(1, grps):
            x_copy(h, lax.rem(my_grp + d, grps), my_grp).start()
    for h in range(halves):
        section[h, slot(my_grp), :] = x_ref[:, h * width : (h + 1) * width]

    to_scalars.wait()
    for load in loads:
        load.wait()

    def add_tile(k, total):
        total = total * table[1, k].astype(jnp.float32) + tiles[table[0, k]].astype(jnp.float32)
        sums[k] = total
        return total

    lax.fori_loop(0, count, add_tile, jnp.zeros((side, side), jnp.float32), unroll=4)

    def split_row(r, carry):
        for c in range(grps):
            pair = r * grps + c
            value = sums[table[2, pair]] * table[3, pair].astype(jnp.float32)
            top = value.astype(jnp.bfloat16)
            rest = (value - top.astype(jnp.float32)).astype(jnp.bfloat16)
            high[r, :, c * side : (c + 1) * side] = top
            low[r, :, c * side : (c + 1) * side] = rest
        return carry

    lax.fori_loop(0, loops, split_row, 0)

    for h in range(halves):
        for d in range(1, grps):
            source = lax.rem(my_grp + d, grps)
            x_copy(h, source, source).wait_recv()
        block = section[h]
        for d in range(1, loops + 1):
            r = lax.rem(my_loop + d, loops)
            part = jnp.dot(high[r], block, preferred_element_type=jnp.float32)
            part = part + jnp.dot(low[r], block, preferred_element_type=jnp.float32)
            if d < loops:
                outgoing[h, d - 1] = part.astype(jnp.bfloat16)
                p_copy(h, d, r, my_loop).start()
            else:
                own[h] = part

    mixed = jnp.broadcast_to(bias_ref[...], out_ref.shape)
    for h in range(halves):
        total = own[h]
        for d in range(1, loops):
            source = lax.rem(my_loop + loops - d, loops)
            p_copy(h, d, source, source).wait_recv()
            total = total + incoming[h, source].astype(jnp.float32)
        mixed = mixed + jnp.dot(
            total.astype(jnp.bfloat16), w_ref[h * width : (h + 1) * width, :],
            preferred_element_type=jnp.float32,
        )
    out_ref[...] = jnp.maximum(mixed, 0.0).astype(out_ref.dtype)

    for h in range(halves):
        for d in range(1, grps):
            x_copy(h, lax.rem(my_grp + d, grps), my_grp).wait_send()
        for d in range(1, loops):
            p_copy(h, d, lax.rem(my_loop + d, loops), my_loop).wait_send()


def on_device(loops, grps, adjacency_tiles, row_block, column_block, features, weight, out_bias):
    count, side = adjacency_tiles.shape[0], adjacency_tiles.shape[1]
    feat = features.shape[1]
    halves = feat // LANES
    pieces = 4 if count % 4 == 0 else 1
    vmem = pl.BlockSpec(memory_space=pltpu.VMEM)
    return pl.pallas_call(
        functools.partial(kernel, loops, grps, pieces),
        out_shape=jax.ShapeDtypeStruct((side, weight.shape[1]), jnp.bfloat16),
        in_specs=[pl.BlockSpec(memory_space=pl.ANY)] + [vmem] * 5,
        out_specs=vmem,
        scratch_shapes=[
            pltpu.VMEM((count, side, side), jnp.bfloat16),
            pltpu.VMEM((8, count), jnp.int32),
            pltpu.SMEM((8, count), jnp.int32),
            pltpu.VMEM((count, side, side), jnp.float32),
            pltpu.VMEM((loops, side, grps * side), jnp.bfloat16),
            pltpu.VMEM((loops, side, grps * side), jnp.bfloat16),
            pltpu.VMEM((halves, grps * side, LANES), jnp.bfloat16),
            pltpu.VMEM((halves, loops, side, LANES), jnp.bfloat16),
            pltpu.VMEM((halves, loops, side, LANES), jnp.bfloat16),
            pltpu.VMEM((halves, side, LANES), jnp.float32),
            pltpu.SemaphoreType.DMA((pieces,)),
            pltpu.SemaphoreType.DMA,
            pltpu.SemaphoreType.DMA((halves, grps)),
            pltpu.SemaphoreType.DMA((halves, grps)),
            pltpu.SemaphoreType.DMA((halves, loops)),
            pltpu.SemaphoreType.DMA((halves, loops)),
        ],
        compiler_params=pltpu.CompilerParams(
            collective_id=0, has_side_effects=True, vmem_limit_bytes=VMEM_BYTES
        ),
    )(
        adjacency_tiles, row_block.reshape(1, count), column_block.reshape(1, count),
        features, weight, out_bias.reshape(1, -1),
    )


def solution(mesh):
    loops, grps = mesh.shape["loop"], mesh.shape["grp"]

    def choose(adjacency_tiles, row_block, column_block, features, weight, out_bias):
        count, side = adjacency_tiles.shape[0], adjacency_tiles.shape[1]
        args = (adjacency_tiles, row_block, column_block, features, weight, out_bias)
        fits = loops * grps <= count and count == LANES and side % LANES == 0
        if fits and features.shape[0] == side and features.shape[1] % LANES == 0:
            return on_device(loops, grps, *args)
        return plain(*args)

    in_specs = (
        P(("loop", "grp"), None, None),
        P(("loop", "grp")),
        P(("loop", "grp")),
        P(("loop", "grp"), None),
        P(),
        P(),
    )
    out_specs = P(("loop", "grp"), None)
    return jax.shard_map(
        choose, mesh=mesh, in_specs=in_specs, out_specs=out_specs, check_vma=False
    )
```

```python
import functools

import jax
import jax.numpy as jnp
from jax import lax
from jax.experimental import pallas as pl
from jax.experimental.pallas import tpu as pltpu
from jax.sharding import PartitionSpec as P

LANES = 128
VMEM_BYTES = 64 * 1024 * 1024


def plain(adjacency_tiles, row_block, column_block, features, weight, out_bias):
    tile_size = adjacency_tiles.shape[1]
    feat_width = features.shape[1]
    loop_count = lax.axis_size("loop")
    section_rows = lax.all_gather(features, "grp", axis=0, tiled=True)
    section_blocks = section_rows.reshape(-1, tile_size, feat_width)
    picked = jnp.take(section_blocks, column_block, axis=0)
    products = jnp.einsum(
        "tij,tjf->tif", adjacency_tiles, picked, preferred_element_type=jnp.float32
    )
    partial_value = jax.ops.segment_sum(products, row_block, num_segments=loop_count)
    received = lax.all_to_all(partial_value, "loop", split_axis=0, concat_axis=0, tiled=True)
    summed = jnp.sum(received, axis=0)
    aggregate = summed.astype(jnp.bfloat16)
    mixed = jnp.dot(aggregate, weight, preferred_element_type=jnp.float32) + out_bias
    return jax.nn.relu(mixed).astype(jnp.bfloat16)


def column_sum(mask, value):
    return jnp.sum(jnp.where(mask, value, 0), axis=0, keepdims=True)


def sort_tables(key, count):
    wide = jnp.broadcast_to(key, (count, count))
    tall = wide.T
    sub = lax.broadcasted_iota(jnp.int32, (count, count), 0)
    lane = lax.broadcasted_iota(jnp.int32, (count, count), 1)
    equal_before = column_sum((tall == wide) & (sub < lane), 1)
    place = column_sum(tall < wide, 1) + equal_before
    place_tall = jnp.broadcast_to(place, (count, count)).T
    joins_tall = jnp.broadcast_to(equal_before, (count, count)).T
    here = place_tall == lane
    order = column_sum(here, sub)
    joins = column_sum(here & (joins_tall > 0), 1)
    last = jnp.maximum(column_sum(tall <= lane, 1) - 1, 0)
    present = jnp.minimum(column_sum(tall == lane, 1), 1)
    return order, joins, last, present


def kernel(
    loops, grps, pieces,
    tiles_hbm, row_hbm, col_hbm, x_ref, w_hbm, bias_hbm, out_ref,
    row_ref, col_ref, w_ref, bias_ref, tiles, table_vec, table, sums, high, low, section, outgoing, incoming, own,
    in_sem, own_sem, tile_sem, table_sem, xs_sem, xr_sem, ps_sem, pr_sem,
):
    count, side = tiles.shape[0], tiles.shape[1]
    halves = section.shape[0]
    width = section.shape[2]
    my_loop, my_grp = lax.axis_index("loop"), lax.axis_index("grp")
    step = count // pieces

    small = [
        pltpu.make_async_copy(source, target, in_sem.at[i])
        for i, (source, target) in enumerate(
            ((row_hbm, row_ref), (col_hbm, col_ref), (w_hbm, w_ref), (bias_hbm, bias_ref))
        )
    ]
    small[0].start()
    small[1].start()
    loads = []
    for i in range(pieces):
        span = pl.ds(i * step, step)
        loads.append(pltpu.make_async_copy(tiles_hbm.at[span], tiles.at[span], tile_sem.at[i]))
        loads[-1].start()

    barrier = pltpu.get_barrier_semaphore()
    for d in range(1, grps):
        pl.semaphore_signal(
            barrier, inc=1, device_id=(my_loop, lax.rem(my_grp + d, grps)),
            device_id_type=pl.DeviceIdType.MESH,
        )
    for d in range(1, loops):
        pl.semaphore_signal(
            barrier, inc=1, device_id=(lax.rem(my_loop + d, loops), my_grp),
            device_id_type=pl.DeviceIdType.MESH,
        )

    small[0].wait()
    small[1].wait()
    rows = sort_tables(row_ref[...] * grps + col_ref[...], count)
    for i, values in enumerate(rows):
        table_vec[i : i + 1, :] = values
    to_scalars = pltpu.make_async_copy(table_vec, table, table_sem)
    to_scalars.start()

    pl.semaphore_wait(barrier, grps + loops - 2)

    def slot(g):
        return pl.ds(pl.multiple_of(g * side, side), side)

    def x_copy(h, target, source):
        return pltpu.make_async_remote_copy(
            src_ref=x_ref.at[:, pl.ds(h * width, width)],
            dst_ref=section.at[h, slot(source)],
            send_sem=xs_sem.at[h, target],
            recv_sem=xr_sem.at[h, source],
            device_id=(my_loop, target),
            device_id_type=pl.DeviceIdType.MESH,
        )

    def p_copy(h, d, target, source):
        return pltpu.make_async_remote_copy(
            src_ref=outgoing.at[h, d - 1],
            dst_ref=incoming.at[h, source],
            send_sem=ps_sem.at[h, d - 1],
            recv_sem=pr_sem.at[h, source],
            device_id=(target, my_grp),
            device_id_type=pl.DeviceIdType.MESH,
        )

    for h in range(halves):
        for d in range(1, grps):
            x_copy(h, lax.rem(my_grp + d, grps), my_grp).start()
    mine = [
        pltpu.make_async_copy(
            x_ref.at[:, pl.ds(h * width, width)], section.at[h, slot(my_grp)], own_sem.at[h]
        )
        for h in range(halves)
    ]
    for copy in mine + small[2:]:
        copy.start()

    to_scalars.wait()
    for load in loads:
        load.wait()

    def add_tile(k, total):
        total = total * table[1, k].astype(jnp.float32) + tiles[table[0, k]].astype(jnp.float32)
        sums[k] = total
        return total

    lax.fori_loop(0, count, add_tile, jnp.zeros((side, side), jnp.float32), unroll=4)

    def split_row(r, carry):
        for c in range(grps):
            pair = r * grps + c
            value = sums[table[2, pair]] * table[3, pair].astype(jnp.float32)
            top = value.astype(jnp.bfloat16)
            rest = (value - top.astype(jnp.float32)).astype(jnp.bfloat16)
            high[r, :, c * side : (c + 1) * side] = top
            low[r, :, c * side : (c + 1) * side] = rest
        return carry

    lax.fori_loop(0, loops, split_row, 0)

    for h in range(halves):
        for d in range(1, grps):
            source = lax.rem(my_grp + d, grps)
            x_copy(h, source, source).wait_recv()
        mine[h].wait()
        block = section[h]
        for d in range(1, loops + 1):
            r = lax.rem(my_loop + d, loops)
            part = jnp.dot(high[r], block, preferred_element_type=jnp.float32)
            part = part + jnp.dot(low[r], block, preferred_element_type=jnp.float32)
            if d < loops:
                outgoing[h, d - 1] = part.astype(jnp.bfloat16)
                p_copy(h, d, r, my_loop).start()
            else:
                own[h] = part

    small[2].wait()
    small[3].wait()
    mixed = jnp.broadcast_to(bias_ref[...], out_ref.shape)
    for h in range(halves):
        total = own[h]
        for d in range(1, loops):
            source = lax.rem(my_loop + loops - d, loops)
            p_copy(h, d, source, source).wait_recv()
            total = total + incoming[h, source].astype(jnp.float32)
        mixed = mixed + jnp.dot(
            total.astype(jnp.bfloat16), w_ref[h * width : (h + 1) * width, :],
            preferred_element_type=jnp.float32,
        )
    out_ref[...] = jnp.maximum(mixed, 0.0).astype(out_ref.dtype)

    for h in range(halves):
        for d in range(1, grps):
            x_copy(h, lax.rem(my_grp + d, grps), my_grp).wait_send()
        for d in range(1, loops):
            p_copy(h, d, lax.rem(my_loop + d, loops), my_loop).wait_send()


def on_device(loops, grps, adjacency_tiles, row_block, column_block, features, weight, out_bias):
    count, side = adjacency_tiles.shape[0], adjacency_tiles.shape[1]
    feat = features.shape[1]
    halves = feat // LANES
    pieces = 4 if count % 4 == 0 else 1
    vmem = pl.BlockSpec(memory_space=pltpu.VMEM)
    return pl.pallas_call(
        functools.partial(kernel, loops, grps, pieces),
        out_shape=jax.ShapeDtypeStruct((side, weight.shape[1]), jnp.bfloat16),
        in_specs=[pl.BlockSpec(memory_space=pl.ANY)] * 6,
        out_specs=vmem,
        scratch_shapes=[
            pltpu.VMEM((1, count), jnp.int32),
            pltpu.VMEM((1, count), jnp.int32),
            pltpu.VMEM(weight.shape, weight.dtype),
            pltpu.VMEM((1, weight.shape[1]), out_bias.dtype),
            pltpu.VMEM((count, side, side), jnp.bfloat16),
            pltpu.VMEM((8, count), jnp.int32),
            pltpu.SMEM((8, count), jnp.int32),
            pltpu.VMEM((count, side, side), jnp.float32),
            pltpu.VMEM((loops, side, grps * side), jnp.bfloat16),
            pltpu.VMEM((loops, side, grps * side), jnp.bfloat16),
            pltpu.VMEM((halves, grps * side, LANES), jnp.bfloat16),
            pltpu.VMEM((halves, loops, side, LANES), jnp.bfloat16),
            pltpu.VMEM((halves, loops, side, LANES), jnp.bfloat16),
            pltpu.VMEM((halves, side, LANES), jnp.float32),
            pltpu.SemaphoreType.DMA((4,)),
            pltpu.SemaphoreType.DMA((halves,)),
            pltpu.SemaphoreType.DMA((pieces,)),
            pltpu.SemaphoreType.DMA,
            pltpu.SemaphoreType.DMA((halves, grps)),
            pltpu.SemaphoreType.DMA((halves, grps)),
            pltpu.SemaphoreType.DMA((halves, loops)),
            pltpu.SemaphoreType.DMA((halves, loops)),
        ],
        compiler_params=pltpu.CompilerParams(
            collective_id=0, has_side_effects=True, vmem_limit_bytes=VMEM_BYTES
        ),
    )(
        adjacency_tiles, row_block.reshape(1, count), column_block.reshape(1, count),
        features, weight, out_bias.reshape(1, -1),
    )


def solution(mesh):
    loops, grps = mesh.shape["loop"], mesh.shape["grp"]

    def choose(adjacency_tiles, row_block, column_block, features, weight, out_bias):
        count, side = adjacency_tiles.shape[0], adjacency_tiles.shape[1]
        args = (adjacency_tiles, row_block, column_block, features, weight, out_bias)
        fits = loops * grps <= count and count == LANES and side % LANES == 0
        if fits and features.shape[0] == side and features.shape[1] % LANES == 0:
            return on_device(loops, grps, *args)
        return plain(*args)

    in_specs = (
        P(("loop", "grp"), None, None),
        P(("loop", "grp")),
        P(("loop", "grp")),
        P(("loop", "grp"), None),
        P(),
        P(),
    )
    out_specs = P(("loop", "grp"), None)
    return jax.shard_map(
        choose, mesh=mesh, in_specs=in_specs, out_specs=out_specs, check_vma=False
    )
```

```python
import functools

import jax
import jax.numpy as jnp
from jax import lax
from jax.experimental import pallas as pl
from jax.experimental.pallas import tpu as pltpu
from jax.sharding import PartitionSpec as P

LANES = 128
VMEM_BYTES = 64 * 1024 * 1024


def plain(adjacency_tiles, row_block, column_block, features, weight, out_bias):
    tile_size = adjacency_tiles.shape[1]
    feat_width = features.shape[1]
    loop_count = lax.axis_size("loop")
    section_rows = lax.all_gather(features, "grp", axis=0, tiled=True)
    section_blocks = section_rows.reshape(-1, tile_size, feat_width)
    picked = jnp.take(section_blocks, column_block, axis=0)
    products = jnp.einsum(
        "tij,tjf->tif", adjacency_tiles, picked, preferred_element_type=jnp.float32
    )
    partial_value = jax.ops.segment_sum(products, row_block, num_segments=loop_count)
    received = lax.all_to_all(partial_value, "loop", split_axis=0, concat_axis=0, tiled=True)
    summed = jnp.sum(received, axis=0)
    aggregate = summed.astype(jnp.bfloat16)
    mixed = jnp.dot(aggregate, weight, preferred_element_type=jnp.float32) + out_bias
    return jax.nn.relu(mixed).astype(jnp.bfloat16)


def column_sum(mask, value):
    return jnp.sum(jnp.where(mask, value, 0), axis=0, keepdims=True)


def sort_tables(key, count):
    wide = jnp.broadcast_to(key, (count, count))
    tall = wide.T
    sub = lax.broadcasted_iota(jnp.int32, (count, count), 0)
    lane = lax.broadcasted_iota(jnp.int32, (count, count), 1)
    equal_before = column_sum((tall == wide) & (sub < lane), 1)
    place = column_sum(tall < wide, 1) + equal_before
    place_tall = jnp.broadcast_to(place, (count, count)).T
    joins_tall = jnp.broadcast_to(equal_before, (count, count)).T
    here = place_tall == lane
    order = column_sum(here, sub)
    joins = column_sum(here & (joins_tall > 0), 1)
    last = jnp.maximum(column_sum(tall <= lane, 1) - 1, 0)
    present = jnp.minimum(column_sum(tall == lane, 1), 1)
    return order, joins, last, present


def kernel(
    loops, grps, pieces,
    tiles_hbm, row_hbm, col_hbm, x_ref, w_hbm, bias_hbm, out_ref,
    row_ref, col_ref, w_ref, bias_ref, tiles, table_vec, table, sums, high, low, section, outgoing, incoming, own,
    in_sem, own_sem, tile_sem, table_sem, xs_sem, xr_sem, ps_sem, pr_sem,
):
    count, side = tiles.shape[0], tiles.shape[1]
    halves = section.shape[0]
    width = section.shape[2]
    my_loop, my_grp = lax.axis_index("loop"), lax.axis_index("grp")
    chips = loops // 2
    my_chip, my_core = lax.div(my_loop, 2), lax.rem(my_loop, 2)
    sibling = 2 * my_chip + 1 - my_core
    step = count // pieces

    small = [
        pltpu.make_async_copy(source, target, in_sem.at[i])
        for i, (source, target) in enumerate(
            ((row_hbm, row_ref), (col_hbm, col_ref), (w_hbm, w_ref), (bias_hbm, bias_ref))
        )
    ]
    small[0].start()
    small[1].start()
    loads = []
    for i in range(pieces):
        span = pl.ds(i * step, step)
        loads.append(pltpu.make_async_copy(tiles_hbm.at[span], tiles.at[span], tile_sem.at[i]))
        loads[-1].start()

    barrier = pltpu.get_barrier_semaphore()
    for d in range(1, grps):
        pl.semaphore_signal(
            barrier, inc=1, device_id=(my_loop, lax.rem(my_grp + d, grps)),
            device_id_type=pl.DeviceIdType.MESH,
        )
    pl.semaphore_signal(
        barrier, inc=1, device_id=(sibling, my_grp), device_id_type=pl.DeviceIdType.MESH
    )
    for d in range(1, chips):
        pl.semaphore_signal(
            barrier, inc=1, device_id=(2 * lax.rem(my_chip + d, chips) + my_core, my_grp),
            device_id_type=pl.DeviceIdType.MESH,
        )

    small[0].wait()
    small[1].wait()
    rows = sort_tables(row_ref[...] * grps + col_ref[...], count)
    for i, values in enumerate(rows):
        table_vec[i : i + 1, :] = values
    to_scalars = pltpu.make_async_copy(table_vec, table, table_sem)
    to_scalars.start()

    pl.semaphore_wait(barrier, grps + chips - 1)

    def slot(g):
        return pl.ds(pl.multiple_of(g * side, side), side)

    def x_copy(h, target, source):
        return pltpu.make_async_remote_copy(
            src_ref=x_ref.at[:, pl.ds(h * width, width)],
            dst_ref=section.at[h, slot(source)],
            send_sem=xs_sem.at[h, target],
            recv_sem=xr_sem.at[h, source],
            device_id=(my_loop, target),
            device_id_type=pl.DeviceIdType.MESH,
        )

    def p_copy(h, d, target, source):
        return pltpu.make_async_remote_copy(
            src_ref=outgoing.at[h, chips + d - 1],
            dst_ref=incoming.at[h, chips + source],
            send_sem=ps_sem.at[h, chips + d - 1],
            recv_sem=pr_sem.at[h, chips + source],
            device_id=(2 * target + my_core, my_grp),
            device_id_type=pl.DeviceIdType.MESH,
        )

    def s_copy(h, d):
        return pltpu.make_async_remote_copy(
            src_ref=outgoing.at[h, d - 1],
            dst_ref=incoming.at[h, d - 1],
            send_sem=ps_sem.at[h, d - 1],
            recv_sem=pr_sem.at[h, d - 1],
            device_id=(sibling, my_grp),
            device_id_type=pl.DeviceIdType.MESH,
        )

    def product(r, block):
        part = jnp.dot(high[r], block, preferred_element_type=jnp.float32)
        return part + jnp.dot(low[r], block, preferred_element_type=jnp.float32)

    for h in range(halves):
        for d in range(1, grps):
            x_copy(h, lax.rem(my_grp + d, grps), my_grp).start()
    mine = [
        pltpu.make_async_copy(
            x_ref.at[:, pl.ds(h * width, width)], section.at[h, slot(my_grp)], own_sem.at[h]
        )
        for h in range(halves)
    ]
    for copy in mine + small[2:]:
        copy.start()

    to_scalars.wait()
    for load in loads:
        load.wait()

    def add_tile(k, total):
        total = total * table[1, k].astype(jnp.float32) + tiles[table[0, k]].astype(jnp.float32)
        sums[k] = total
        return total

    lax.fori_loop(0, count, add_tile, jnp.zeros((side, side), jnp.float32), unroll=4)

    def split_row(r, carry):
        for c in range(grps):
            pair = r * grps + c
            value = sums[table[2, pair]] * table[3, pair].astype(jnp.float32)
            top = value.astype(jnp.bfloat16)
            rest = (value - top.astype(jnp.float32)).astype(jnp.bfloat16)
            high[r, :, c * side : (c + 1) * side] = top
            low[r, :, c * side : (c + 1) * side] = rest
        return carry

    lax.fori_loop(0, loops, split_row, 0)

    for h in range(halves):
        for d in range(1, grps):
            source = lax.rem(my_grp + d, grps)
            x_copy(h, source, source).wait_recv()
        mine[h].wait()
        block = section[h]
        for d in range(1, chips + 1):
            chip = lax.rem(my_chip + d, chips)
            part = product(2 * chip + 1 - my_core, block)
            outgoing[h, d - 1] = part.astype(jnp.bfloat16)
            s_copy(h, d).start()
        for d in range(1, chips + 1):
            chip = lax.rem(my_chip + d, chips)
            part = product(2 * chip + my_core, block)
            s_copy(h, d).wait_recv()
            part = part + incoming[h, d - 1].astype(jnp.float32)
            if d < chips:
                outgoing[h, chips + d - 1] = part.astype(jnp.bfloat16)
                p_copy(h, d, chip, my_chip).start()
            else:
                own[h] = part

    small[2].wait()
    small[3].wait()
    mixed = jnp.broadcast_to(bias_ref[...], out_ref.shape)
    for h in range(halves):
        total = own[h]
        for d in range(1, chips):
            source = lax.rem(my_chip + chips - d, chips)
            p_copy(h, d, source, source).wait_recv()
            total = total + incoming[h, chips + source].astype(jnp.float32)
        mixed = mixed + jnp.dot(
            total.astype(jnp.bfloat16), w_ref[h * width : (h + 1) * width, :],
            preferred_element_type=jnp.float32,
        )
    out_ref[...] = jnp.maximum(mixed, 0.0).astype(out_ref.dtype)

    for h in range(halves):
        for d in range(1, grps):
            x_copy(h, lax.rem(my_grp + d, grps), my_grp).wait_send()
        for d in range(1, chips + 1):
            s_copy(h, d).wait_send()
        for d in range(1, chips):
            p_copy(h, d, lax.rem(my_chip + d, chips), my_chip).wait_send()


def on_device(loops, grps, adjacency_tiles, row_block, column_block, features, weight, out_bias):
    count, side = adjacency_tiles.shape[0], adjacency_tiles.shape[1]
    feat = features.shape[1]
    halves = feat // LANES
    pieces = 4 if count % 4 == 0 else 1
    vmem = pl.BlockSpec(memory_space=pltpu.VMEM)
    return pl.pallas_call(
        functools.partial(kernel, loops, grps, pieces),
        out_shape=jax.ShapeDtypeStruct((side, weight.shape[1]), jnp.bfloat16),
        in_specs=[pl.BlockSpec(memory_space=pl.ANY)] * 6,
        out_specs=vmem,
        scratch_shapes=[
            pltpu.VMEM((1, count), jnp.int32),
            pltpu.VMEM((1, count), jnp.int32),
            pltpu.VMEM(weight.shape, weight.dtype),
            pltpu.VMEM((1, weight.shape[1]), out_bias.dtype),
            pltpu.VMEM((count, side, side), jnp.bfloat16),
            pltpu.VMEM((8, count), jnp.int32),
            pltpu.SMEM((8, count), jnp.int32),
            pltpu.VMEM((count, side, side), jnp.float32),
            pltpu.VMEM((loops, side, grps * side), jnp.bfloat16),
            pltpu.VMEM((loops, side, grps * side), jnp.bfloat16),
            pltpu.VMEM((halves, grps * side, LANES), jnp.bfloat16),
            pltpu.VMEM((halves, loops, side, LANES), jnp.bfloat16),
            pltpu.VMEM((halves, loops, side, LANES), jnp.bfloat16),
            pltpu.VMEM((halves, side, LANES), jnp.float32),
            pltpu.SemaphoreType.DMA((4,)),
            pltpu.SemaphoreType.DMA((halves,)),
            pltpu.SemaphoreType.DMA((pieces,)),
            pltpu.SemaphoreType.DMA,
            pltpu.SemaphoreType.DMA((halves, grps)),
            pltpu.SemaphoreType.DMA((halves, grps)),
            pltpu.SemaphoreType.DMA((halves, loops)),
            pltpu.SemaphoreType.DMA((halves, loops)),
        ],
        compiler_params=pltpu.CompilerParams(
            collective_id=0, has_side_effects=True, vmem_limit_bytes=VMEM_BYTES
        ),
    )(
        adjacency_tiles, row_block.reshape(1, count), column_block.reshape(1, count),
        features, weight, out_bias.reshape(1, -1),
    )


def solution(mesh):
    loops, grps = mesh.shape["loop"], mesh.shape["grp"]

    def choose(adjacency_tiles, row_block, column_block, features, weight, out_bias):
        count, side = adjacency_tiles.shape[0], adjacency_tiles.shape[1]
        args = (adjacency_tiles, row_block, column_block, features, weight, out_bias)
        fits = loops % 2 == 0 and loops * grps <= count and count == LANES and side % LANES == 0
        if fits and features.shape[0] == side and features.shape[1] % LANES == 0:
            return on_device(loops, grps, *args)
        return plain(*args)

    in_specs = (
        P(("loop", "grp"), None, None),
        P(("loop", "grp")),
        P(("loop", "grp")),
        P(("loop", "grp"), None),
        P(),
        P(),
    )
    out_specs = P(("loop", "grp"), None)
    return jax.shard_map(
        choose, mesh=mesh, in_specs=in_specs, out_specs=out_specs, check_vma=False
    )
```

```python
import functools

import jax
import jax.numpy as jnp
from jax import lax
from jax.experimental import pallas as pl
from jax.experimental.pallas import tpu as pltpu
from jax.sharding import PartitionSpec as P

LANES = 128
VMEM_BYTES = 64 * 1024 * 1024


def plain(adjacency_tiles, row_block, column_block, features, weight, out_bias):
    tile_size = adjacency_tiles.shape[1]
    feat_width = features.shape[1]
    loop_count = lax.axis_size("loop")
    section_rows = lax.all_gather(features, "grp", axis=0, tiled=True)
    section_blocks = section_rows.reshape(-1, tile_size, feat_width)
    picked = jnp.take(section_blocks, column_block, axis=0)
    products = jnp.einsum(
        "tij,tjf->tif", adjacency_tiles, picked, preferred_element_type=jnp.float32
    )
    partial_value = jax.ops.segment_sum(products, row_block, num_segments=loop_count)
    received = lax.all_to_all(partial_value, "loop", split_axis=0, concat_axis=0, tiled=True)
    summed = jnp.sum(received, axis=0)
    aggregate = summed.astype(jnp.bfloat16)
    mixed = jnp.dot(aggregate, weight, preferred_element_type=jnp.float32) + out_bias
    return jax.nn.relu(mixed).astype(jnp.bfloat16)


def column_sum(mask, value):
    return jnp.sum(jnp.where(mask, value, 0), axis=0, keepdims=True)


def sort_tables(key, count):
    wide = jnp.broadcast_to(key, (count, count))
    tall = wide.T
    sub = lax.broadcasted_iota(jnp.int32, (count, count), 0)
    lane = lax.broadcasted_iota(jnp.int32, (count, count), 1)
    equal_before = column_sum((tall == wide) & (sub < lane), 1)
    place = column_sum(tall < wide, 1) + equal_before
    place_tall = jnp.broadcast_to(place, (count, count)).T
    joins_tall = jnp.broadcast_to(equal_before, (count, count)).T
    here = place_tall == lane
    order = column_sum(here, sub)
    joins = column_sum(here & (joins_tall > 0), 1)
    last = jnp.maximum(column_sum(tall <= lane, 1) - 1, 0)
    present = jnp.minimum(column_sum(tall == lane, 1), 1)
    return order, joins, last, present


def kernel(
    loops, grps, pieces,
    tiles_hbm, row_hbm, col_hbm, x_ref, w_hbm, bias_hbm, out_ref,
    row_ref, col_ref, w_ref, bias_ref, tiles, table_vec, table, sums, high, low, section, outgoing, incoming, own,
    in_sem, own_sem, tile_sem, table_sem, xs_sem, xr_sem, ps_sem, pr_sem,
):
    count, side = tiles.shape[0], tiles.shape[1]
    halves = section.shape[0]
    width = section.shape[2]
    my_loop, my_grp = lax.axis_index("loop"), lax.axis_index("grp")
    step = count // pieces

    small = [
        pltpu.make_async_copy(source, target, in_sem.at[i])
        for i, (source, target) in enumerate(
            ((row_hbm, row_ref), (col_hbm, col_ref), (w_hbm, w_ref), (bias_hbm, bias_ref))
        )
    ]
    small[0].start()
    small[1].start()
    loads = []
    for i in range(pieces):
        span = pl.ds(i * step, step)
        loads.append(pltpu.make_async_copy(tiles_hbm.at[span], tiles.at[span], tile_sem.at[i]))
        loads[-1].start()

    barrier = pltpu.get_barrier_semaphore()
    for d in range(1, grps):
        pl.semaphore_signal(
            barrier, inc=1, device_id=(my_loop, lax.rem(my_grp + d, grps)),
            device_id_type=pl.DeviceIdType.MESH,
        )
    for d in range(1, loops):
        pl.semaphore_signal(
            barrier, inc=1, device_id=(lax.rem(my_loop + d, loops), my_grp),
            device_id_type=pl.DeviceIdType.MESH,
        )

    small[0].wait()
    small[1].wait()
    rows = sort_tables(row_ref[...] * grps + col_ref[...], count)
    for i, values in enumerate(rows):
        table_vec[i : i + 1, :] = values
    to_scalars = pltpu.make_async_copy(table_vec, table, table_sem)
    to_scalars.start()

    pl.semaphore_wait(barrier, grps + loops - 2)

    def slot(g):
        return pl.ds(pl.multiple_of(g * side, side), side)

    def x_copy(h, target, source):
        return pltpu.make_async_remote_copy(
            src_ref=x_ref.at[:, pl.ds(h * width, width)],
            dst_ref=section.at[h, slot(source)],
            send_sem=xs_sem.at[h, target],
            recv_sem=xr_sem.at[h, source],
            device_id=(my_loop, target),
            device_id_type=pl.DeviceIdType.MESH,
        )

    def p_copy(h, d, target, source):
        return pltpu.make_async_remote_copy(
            src_ref=outgoing.at[h, d - 1],
            dst_ref=incoming.at[h, source],
            send_sem=ps_sem.at[h, d - 1],
            recv_sem=pr_sem.at[h, source],
            device_id=(target, my_grp),
            device_id_type=pl.DeviceIdType.MESH,
        )

    for h in range(halves):
        for d in range(1, grps):
            x_copy(h, lax.rem(my_grp + d, grps), my_grp).start()
    mine = [
        pltpu.make_async_copy(
            x_ref.at[:, pl.ds(h * width, width)], section.at[h, slot(my_grp)], own_sem.at[h]
        )
        for h in range(halves)
    ]
    for copy in mine + small[2:]:
        copy.start()

    to_scalars.wait()
    for load in loads:
        load.wait()

    def add_tile(k, total):
        total = total * table[1, k].astype(jnp.float32) + tiles[table[0, k]].astype(jnp.float32)
        sums[k] = total
        return total

    lax.fori_loop(0, count, add_tile, jnp.zeros((side, side), jnp.float32), unroll=4)

    def split_row(r, carry):
        for c in range(grps):
            pair = r * grps + c
            value = sums[table[2, pair]] * table[3, pair].astype(jnp.float32)
            top = value.astype(jnp.bfloat16)
            rest = (value - top.astype(jnp.float32)).astype(jnp.bfloat16)
            high[r, :, c * side : (c + 1) * side] = top
            low[r, :, c * side : (c + 1) * side] = rest
        return carry

    lax.fori_loop(0, loops, split_row, 0)

    for h in range(halves):
        for d in range(1, grps):
            source = lax.rem(my_grp + d, grps)
            x_copy(h, source, source).wait_recv()
        mine[h].wait()
        block = section[h]
        for d in range(1, loops + 1):
            r = lax.rem(my_loop + d, loops)
            part = jnp.dot(high[r], block, preferred_element_type=jnp.float32)
            part = part + jnp.dot(low[r], block, preferred_element_type=jnp.float32)
            if d < loops:
                outgoing[h, d - 1] = part.astype(jnp.bfloat16)
                p_copy(h, d, r, my_loop).start()
            else:
                own[h] = part

    small[2].wait()
    small[3].wait()
    mixed = jnp.broadcast_to(bias_ref[...], out_ref.shape)
    for h in range(halves):
        total = own[h]
        for d in range(1, loops):
            source = lax.rem(my_loop + loops - d, loops)
            p_copy(h, d, source, source).wait_recv()
            total = total + incoming[h, source].astype(jnp.float32)
        mixed = mixed + jnp.dot(
            total.astype(jnp.bfloat16), w_ref[h * width : (h + 1) * width, :],
            preferred_element_type=jnp.float32,
        )
    out_ref[...] = jnp.maximum(mixed, 0.0).astype(out_ref.dtype)

    for h in range(halves):
        for d in range(1, grps):
            x_copy(h, lax.rem(my_grp + d, grps), my_grp).wait_send()
        for d in range(1, loops):
            p_copy(h, d, lax.rem(my_loop + d, loops), my_loop).wait_send()


def on_device(loops, grps, adjacency_tiles, row_block, column_block, features, weight, out_bias):
    count, side = adjacency_tiles.shape[0], adjacency_tiles.shape[1]
    feat = features.shape[1]
    halves = 1
    width = feat // halves
    pieces = 4 if count % 4 == 0 else 1
    vmem = pl.BlockSpec(memory_space=pltpu.VMEM)
    return pl.pallas_call(
        functools.partial(kernel, loops, grps, pieces),
        out_shape=jax.ShapeDtypeStruct((side, weight.shape[1]), jnp.bfloat16),
        in_specs=[pl.BlockSpec(memory_space=pl.ANY)] * 6,
        out_specs=vmem,
        scratch_shapes=[
            pltpu.VMEM((1, count), jnp.int32),
            pltpu.VMEM((1, count), jnp.int32),
            pltpu.VMEM(weight.shape, weight.dtype),
            pltpu.VMEM((1, weight.shape[1]), out_bias.dtype),
            pltpu.VMEM((count, side, side), jnp.bfloat16),
            pltpu.VMEM((8, count), jnp.int32),
            pltpu.SMEM((8, count), jnp.int32),
            pltpu.VMEM((count, side, side), jnp.float32),
            pltpu.VMEM((loops, side, grps * side), jnp.bfloat16),
            pltpu.VMEM((loops, side, grps * side), jnp.bfloat16),
            pltpu.VMEM((halves, grps * side, width), jnp.bfloat16),
            pltpu.VMEM((halves, loops, side, width), jnp.bfloat16),
            pltpu.VMEM((halves, loops, side, width), jnp.bfloat16),
            pltpu.VMEM((halves, side, width), jnp.float32),
            pltpu.SemaphoreType.DMA((4,)),
            pltpu.SemaphoreType.DMA((halves,)),
            pltpu.SemaphoreType.DMA((pieces,)),
            pltpu.SemaphoreType.DMA,
            pltpu.SemaphoreType.DMA((halves, grps)),
            pltpu.SemaphoreType.DMA((halves, grps)),
            pltpu.SemaphoreType.DMA((halves, loops)),
            pltpu.SemaphoreType.DMA((halves, loops)),
        ],
        compiler_params=pltpu.CompilerParams(
            collective_id=0, has_side_effects=True, vmem_limit_bytes=VMEM_BYTES
        ),
    )(
        adjacency_tiles, row_block.reshape(1, count), column_block.reshape(1, count),
        features, weight, out_bias.reshape(1, -1),
    )


def solution(mesh):
    loops, grps = mesh.shape["loop"], mesh.shape["grp"]

    def choose(adjacency_tiles, row_block, column_block, features, weight, out_bias):
        count, side = adjacency_tiles.shape[0], adjacency_tiles.shape[1]
        args = (adjacency_tiles, row_block, column_block, features, weight, out_bias)
        fits = loops * grps <= count and count == LANES and side % LANES == 0
        if fits and features.shape[0] == side and features.shape[1] % LANES == 0:
            return on_device(loops, grps, *args)
        return plain(*args)

    in_specs = (
        P(("loop", "grp"), None, None),
        P(("loop", "grp")),
        P(("loop", "grp")),
        P(("loop", "grp"), None),
        P(),
        P(),
    )
    out_specs = P(("loop", "grp"), None)
    return jax.shard_map(
        choose, mesh=mesh, in_specs=in_specs, out_specs=out_specs, check_vma=False
    )
```

```python
import functools

import jax
import jax.numpy as jnp
from jax import lax
from jax.experimental import pallas as pl
from jax.experimental.pallas import tpu as pltpu
from jax.sharding import PartitionSpec as P

LANES = 128
VMEM_BYTES = 64 * 1024 * 1024


def plain(adjacency_tiles, row_block, column_block, features, weight, out_bias):
    tile_size = adjacency_tiles.shape[1]
    feat_width = features.shape[1]
    loop_count = lax.axis_size("loop")
    section_rows = lax.all_gather(features, "grp", axis=0, tiled=True)
    section_blocks = section_rows.reshape(-1, tile_size, feat_width)
    picked = jnp.take(section_blocks, column_block, axis=0)
    products = jnp.einsum(
        "tij,tjf->tif", adjacency_tiles, picked, preferred_element_type=jnp.float32
    )
    partial_value = jax.ops.segment_sum(products, row_block, num_segments=loop_count)
    received = lax.all_to_all(partial_value, "loop", split_axis=0, concat_axis=0, tiled=True)
    summed = jnp.sum(received, axis=0)
    aggregate = summed.astype(jnp.bfloat16)
    mixed = jnp.dot(aggregate, weight, preferred_element_type=jnp.float32) + out_bias
    return jax.nn.relu(mixed).astype(jnp.bfloat16)


def column_sum(mask, value):
    return jnp.sum(jnp.where(mask, value, 0), axis=0, keepdims=True)


def sort_tables(key, count):
    wide = jnp.broadcast_to(key, (count, count))
    tall = wide.T
    sub = lax.broadcasted_iota(jnp.int32, (count, count), 0)
    lane = lax.broadcasted_iota(jnp.int32, (count, count), 1)
    equal_before = column_sum((tall == wide) & (sub < lane), 1)
    place = column_sum(tall < wide, 1) + equal_before
    place_tall = jnp.broadcast_to(place, (count, count)).T
    joins_tall = jnp.broadcast_to(equal_before, (count, count)).T
    here = place_tall == lane
    order = column_sum(here, sub)
    joins = column_sum(here & (joins_tall > 0), 1)
    last = jnp.maximum(column_sum(tall <= lane, 1) - 1, 0)
    present = jnp.minimum(column_sum(tall == lane, 1), 1)
    return order, joins, last, present


def kernel(
    loops, grps, pieces,
    tiles_hbm, row_hbm, col_hbm, x_ref, w_hbm, bias_hbm, out_ref,
    row_ref, col_ref, w_ref, bias_ref, tiles, table_vec, table, sums, high, low, section, outgoing, incoming, own,
    in_sem, own_sem, tile_sem, table_sem, xs_sem, xr_sem, ps_sem, pr_sem,
):
    count, side = tiles.shape[0], tiles.shape[1]
    halves = section.shape[0]
    width = section.shape[2]
    my_loop, my_grp = lax.axis_index("loop"), lax.axis_index("grp")
    step = count // pieces

    small = [
        pltpu.make_async_copy(source, target, in_sem.at[i])
        for i, (source, target) in enumerate(
            ((row_hbm, row_ref), (col_hbm, col_ref), (w_hbm, w_ref), (bias_hbm, bias_ref))
        )
    ]
    small[0].start()
    small[1].start()
    loads = []
    for i in range(pieces):
        span = pl.ds(i * step, step)
        loads.append(pltpu.make_async_copy(tiles_hbm.at[span], tiles.at[span], tile_sem.at[i]))
        loads[-1].start()

    barrier = pltpu.get_barrier_semaphore()
    for d in range(1, grps):
        pl.semaphore_signal(
            barrier, inc=1, device_id=(my_loop, lax.rem(my_grp + d, grps)),
            device_id_type=pl.DeviceIdType.MESH,
        )
    for d in range(1, loops):
        pl.semaphore_signal(
            barrier, inc=1, device_id=(lax.rem(my_loop + d, loops), my_grp),
            device_id_type=pl.DeviceIdType.MESH,
        )

    small[0].wait()
    small[1].wait()
    rows = sort_tables(row_ref[...] * grps + col_ref[...], count)
    for i, values in enumerate(rows):
        table_vec[i : i + 1, :] = values
    to_scalars = pltpu.make_async_copy(table_vec, table, table_sem)
    to_scalars.start()

    pl.semaphore_wait(barrier, grps + loops - 2)

    def slot(g):
        return pl.ds(pl.multiple_of(g * side, side), side)

    def x_copy(h, target, source):
        return pltpu.make_async_remote_copy(
            src_ref=x_ref.at[:, pl.ds(h * width, width)],
            dst_ref=section.at[h, slot(source)],
            send_sem=xs_sem.at[h, target],
            recv_sem=xr_sem.at[h, source],
            device_id=(my_loop, target),
            device_id_type=pl.DeviceIdType.MESH,
        )

    def p_copy(h, d, target, source):
        return pltpu.make_async_remote_copy(
            src_ref=outgoing.at[h, d - 1],
            dst_ref=incoming.at[h, source],
            send_sem=ps_sem.at[h, d - 1],
            recv_sem=pr_sem.at[h, source],
            device_id=(target, my_grp),
            device_id_type=pl.DeviceIdType.MESH,
        )

    for h in range(halves):
        for d in range(1, grps):
            x_copy(h, lax.rem(my_grp + d, grps), my_grp).start()
    mine = [
        pltpu.make_async_copy(
            x_ref.at[:, pl.ds(h * width, width)], section.at[h, slot(my_grp)], own_sem.at[h]
        )
        for h in range(halves)
    ]
    for copy in mine + small[2:]:
        copy.start()

    to_scalars.wait()
    for load in loads:
        load.wait()

    def add_tile(k, total):
        total = total * table[1, k].astype(jnp.float32) + tiles[table[0, k]].astype(jnp.float32)
        sums[k] = total
        return total

    lax.fori_loop(0, count, add_tile, jnp.zeros((side, side), jnp.float32), unroll=4)

    def split_row(r, carry):
        for c in range(grps):
            pair = r * grps + c
            value = sums[table[2, pair]] * table[3, pair].astype(jnp.float32)
            top = value.astype(jnp.bfloat16)
            rest = (value - top.astype(jnp.float32)).astype(jnp.bfloat16)
            high[r, :, c * side : (c + 1) * side] = top
            low[r, :, c * side : (c + 1) * side] = rest
        return carry

    lax.fori_loop(0, loops, split_row, 0)

    for h in range(halves):
        for d in range(1, grps):
            source = lax.rem(my_grp + d, grps)
            x_copy(h, source, source).wait_recv()
        mine[h].wait()
        block = section[h]
        for d in range(1, loops + 1):
            r = lax.rem(my_loop + d, loops)
            part = jnp.dot(high[r], block, preferred_element_type=jnp.float32)
            part = part + jnp.dot(low[r], block, preferred_element_type=jnp.float32)
            if d < loops:
                outgoing[h, d - 1] = part.astype(jnp.bfloat16)
                p_copy(h, d, r, my_loop).start()
            else:
                own[h] = part

    small[2].wait()
    small[3].wait()
    mixed = jnp.broadcast_to(bias_ref[...], out_ref.shape)
    for h in range(halves):
        total = own[h]
        for d in range(1, loops):
            source = lax.rem(my_loop + loops - d, loops)
            p_copy(h, d, source, source).wait_recv()
            total = total + incoming[h, source].astype(jnp.float32)
        mixed = mixed + jnp.dot(
            total.astype(jnp.bfloat16), w_ref[h * width : (h + 1) * width, :],
            preferred_element_type=jnp.float32,
        )
    out_ref[...] = mixed.astype(out_ref.dtype)

    for h in range(halves):
        for d in range(1, grps):
            x_copy(h, lax.rem(my_grp + d, grps), my_grp).wait_send()
        for d in range(1, loops):
            p_copy(h, d, lax.rem(my_loop + d, loops), my_loop).wait_send()


def on_device(loops, grps, adjacency_tiles, row_block, column_block, features, weight, out_bias):
    count, side = adjacency_tiles.shape[0], adjacency_tiles.shape[1]
    feat = features.shape[1]
    halves = feat // LANES
    pieces = 4 if count % 4 == 0 else 1
    vmem = pl.BlockSpec(memory_space=pltpu.VMEM)
    mixed = pl.pallas_call(
        functools.partial(kernel, loops, grps, pieces),
        out_shape=jax.ShapeDtypeStruct((side, weight.shape[1]), jnp.bfloat16),
        in_specs=[pl.BlockSpec(memory_space=pl.ANY)] * 6,
        out_specs=vmem,
        scratch_shapes=[
            pltpu.VMEM((1, count), jnp.int32),
            pltpu.VMEM((1, count), jnp.int32),
            pltpu.VMEM(weight.shape, weight.dtype),
            pltpu.VMEM((1, weight.shape[1]), out_bias.dtype),
            pltpu.VMEM((count, side, side), jnp.bfloat16),
            pltpu.VMEM((8, count), jnp.int32),
            pltpu.SMEM((8, count), jnp.int32),
            pltpu.VMEM((count, side, side), jnp.float32),
            pltpu.VMEM((loops, side, grps * side), jnp.bfloat16),
            pltpu.VMEM((loops, side, grps * side), jnp.bfloat16),
            pltpu.VMEM((halves, grps * side, LANES), jnp.bfloat16),
            pltpu.VMEM((halves, loops, side, LANES), jnp.bfloat16),
            pltpu.VMEM((halves, loops, side, LANES), jnp.bfloat16),
            pltpu.VMEM((halves, side, LANES), jnp.float32),
            pltpu.SemaphoreType.DMA((4,)),
            pltpu.SemaphoreType.DMA((halves,)),
            pltpu.SemaphoreType.DMA((pieces,)),
            pltpu.SemaphoreType.DMA,
            pltpu.SemaphoreType.DMA((halves, grps)),
            pltpu.SemaphoreType.DMA((halves, grps)),
            pltpu.SemaphoreType.DMA((halves, loops)),
            pltpu.SemaphoreType.DMA((halves, loops)),
        ],
        compiler_params=pltpu.CompilerParams(
            collective_id=0, has_side_effects=True, vmem_limit_bytes=VMEM_BYTES
        ),
    )(
        adjacency_tiles, row_block.reshape(1, count), column_block.reshape(1, count),
        features, weight, out_bias.reshape(1, -1),
    )
    return jax.nn.relu(mixed)


def solution(mesh):
    loops, grps = mesh.shape["loop"], mesh.shape["grp"]

    def choose(adjacency_tiles, row_block, column_block, features, weight, out_bias):
        count, side = adjacency_tiles.shape[0], adjacency_tiles.shape[1]
        args = (adjacency_tiles, row_block, column_block, features, weight, out_bias)
        fits = loops * grps <= count and count == LANES and side % LANES == 0
        if fits and features.shape[0] == side and features.shape[1] % LANES == 0:
            return on_device(loops, grps, *args)
        return plain(*args)

    in_specs = (
        P(("loop", "grp"), None, None),
        P(("loop", "grp")),
        P(("loop", "grp")),
        P(("loop", "grp"), None),
        P(),
        P(),
    )
    out_specs = P(("loop", "grp"), None)
    return jax.shard_map(
        choose, mesh=mesh, in_specs=in_specs, out_specs=out_specs, check_vma=False
    )
```
